128 devices in a mesh: dp: 8 (over x, z_lo), mp: 16 (over y, z_hi, core).
Axes of the slice: x: 4, y: 4, z: 4 (z_hi: 2, z_lo: 2; z = z_hi * 2 + z_lo), core: 2. Of those that a mesh axis runs over, the one named last changes fastest.
Arguments:
- out_grads: bfloat16 [1024, 12288], P('dp', 'mp'), may hold values from -48 to 48
- activations: bfloat16 [1024, 3072], P('mp', 'dp'), may hold values from -48 to 48
- factor_a: float32 [3072, 3072], P('dp', 'mp'), may hold values from -6 to 6
- factor_g: float32 [12288, 12288], P('mp', 'dp'), may hold values from -6 to 6
- basis_a: bfloat16 [3072, 3072], P('dp'), may hold values from -0.109375 to 0.109375
- basis_g: bfloat16 [12288, 12288], P('mp', 'dp'), may hold values from -0.0546875 to 0.0546875
- spectrum_a: float32 [3072], P('mp'), may hold values from 0.5 to 4
- spectrum_g: float32 [12288], P('dp'), may hold values from 0.5 to 4
Outputs:
- update: bfloat16 [12288, 3072], P('mp', 'dp')
- factor_a_new: float32 [3072, 3072], P('dp', 'mp')
- factor_g_new: float32 [12288, 12288], P('mp', 'dp')
The draws below stay inside these ranges and needn't reach their ends.
All inputs are finite; a program needn't handle non-finite values.
Results may differ from the reference program's by a relative error of at most 0.028.
Values may be sent and summed in bfloat16 or wider, within the bound.
No kernel may reach another device: no remote copies, remote signals or barrier semaphores. Data moves between devices by JAX's collectives and lax.ppermute only.
A program may use at most 128 MiB of HBM per device.

```python
import math
import jax
import jax.numpy as jnp
from jax import lax

DI = 3072
DO = 12288
TOKENS = 1024


def steps_of(own_key, dims, cuts, least, high):
    factor_of, own = 1.0, jax.random.fold_in(own_key, 6)
    for dim, parts in cuts:
        heights = jnp.exp(jax.random.uniform(jax.random.fold_in(own, dim), (parts,), jnp.float32, least / len(cuts), high / len(cuts)))
        factor_of = factor_of * jnp.repeat(heights, dims[dim] // parts).reshape([-1 if axis == dim else 1 for axis in range(len(dims))])
    return factor_of


def gaussian(own_key, extent, spread, limit, split=(), kind=jnp.bfloat16):
    drawn = jax.random.normal(own_key, extent, jnp.float32) * spread
    if len(split) > 0:
        drawn = steps_of(own_key, extent, split, -0.22, 0.18) * drawn
    return jnp.clip(drawn, min=-limit, max=limit).astype(kind)


def setup_inputs(seed: int = 0) -> dict:
    keys = jax.random.split(jax.random.key(seed), 9)
    return {
        "out_grads": gaussian(keys[0], (TOKENS, DO), 8.0, 48.0, ((0, 8), (1, 16))),
        "activations": gaussian(keys[1], (TOKENS, DI), 8.0, 48.0, ((0, 16), (1, 8))),
        "factor_a": gaussian(keys[2], (DI, DI), 1.0, 6.0, ((0, 8), (1, 16)), jnp.float32),
        "factor_g": gaussian(keys[3], (DO, DO), 1.0, 6.0, ((0, 16), (1, 8)), jnp.float32),
        "basis_a": gaussian(keys[4], (DI, DI), DI ** -0.5, 0.109375, ((0, 8),)),
        "basis_g": gaussian(keys[5], (DO, DO), DO ** -0.5, 0.0546875, ((0, 16), (1, 8))),
        "spectrum_a": jnp.clip(jnp.exp(math.log(4.0) - 2.0794415 * jax.random.uniform(keys[6], (DI,), jnp.float32) ** steps_of(keys[6], (DI,), ((0, 16),), -0.2, 0.2)), 0.5, 4.0),
        "spectrum_g": jnp.clip(jnp.exp(math.log(4.0) - 2.0794415 * jax.random.uniform(keys[7], (DO,), jnp.float32) ** steps_of(keys[7], (DO,), ((0, 8),), -0.2, 0.2)), 0.5, 4.0),
    }


decay_rate = 0.95
damping = 0.25


def contract_rows(left, right):
    return lax.dot_general(left, right, (((0,), (0,)), ((), ())), preferred_element_type=jnp.float32)


def reference(out_grads, activations, factor_a, factor_g, basis_a, basis_g, spectrum_a, spectrum_g):
    projected_g = jnp.dot(out_grads, basis_g, preferred_element_type=jnp.float32).astype(jnp.bfloat16)
    projected_a = jnp.dot(activations, basis_a, preferred_element_type=jnp.float32).astype(jnp.bfloat16)
    rotated = contract_rows(projected_g, projected_a) / TOKENS
    scaled = (rotated / (spectrum_g[:, None] * spectrum_a[None, :] + damping)).astype(jnp.bfloat16)
    back = jnp.dot(basis_g, scaled, preferred_element_type=jnp.float32).astype(jnp.bfloat16)
    update = lax.dot_general(back, basis_a, (((1,), (1,)), ((), ())), preferred_element_type=jnp.float32).astype(jnp.bfloat16)
    factor_a_new = decay_rate * factor_a + ((1.0 - decay_rate) / TOKENS) * contract_rows(activations, activations)
    factor_g_new = decay_rate * factor_g + ((1.0 - decay_rate) / TOKENS) * contract_rows(out_grads, out_grads)
    return update, factor_a_new, factor_g_new
```

```python
import jax
import jax.numpy as jnp
from jax import lax
from jax.sharding import Mesh, PartitionSpec as P

decay_rate = 0.95
damping = 0.25
NAMES = ("x", "zl", "y", "zh", "c")
SIZES = (4, 2, 4, 2, 2)
f32 = jnp.float32
bf16 = jnp.bfloat16


def permute_all(value, target):
    pairs = []
    source = 0
    for x in range(4):
        for zl in range(2):
            for y in range(4):
                for zh in range(2):
                    for c in range(2):
                        tx, tzl, ty, tzh, tc = target(x, zl, y, zh, c)
                        dest = (((tx % 4 * 2 + tzl) * 4 + ty % 4) * 2 + tzh) * 2 + tc
                        pairs.append((source, dest))
                        source += 1
    return lax.ppermute(value, NAMES, pairs)


def flip(value, axis):
    return lax.ppermute(value, axis, [(0, 1), (1, 0)])


def shift(value, axis, by):
    return lax.ppermute(value, axis, [((i + by) % 4, i) for i in range(4)])


def exchange(blocks, axis):
    return lax.all_to_all(blocks, axis, split_axis=0, concat_axis=0, tiled=True)


def spread(block, axis, n):
    return exchange(jnp.broadcast_to(block, (n,) + block.shape), axis)


def dot(a, b):
    return jnp.dot(a, b, preferred_element_type=f32)


def contract_rows(left, right):
    return lax.dot_general(left, right, (((0,), (0,)), ((), ())), preferred_element_type=f32)


def order(index, own, other, axis):
    return jnp.where(
        index == 0,
        jnp.concatenate([own, other], axis=axis),
        jnp.concatenate([other, own], axis=axis),
    )


def shards(out_grads, activations, factor_a, factor_g, basis_a, basis_g, spectrum_a, spectrum_g):
    zl = lax.axis_index("zl")
    zh = lax.axis_index("zh")
    c = lax.axis_index("c")
    tokens = out_grads.shape[0] * 8
    rows, units = out_grads.shape
    tok, feats = activations.shape
    di = basis_a.shape[1]
    half = basis_g.shape[1] // 2
    rate = (1.0 - decay_rate) / tokens

    g_own = lax.dynamic_slice_in_dim(basis_g, c * half, half, 1)
    g_far = lax.dynamic_slice_in_dim(basis_g, (1 - c) * half, half, 1)

    act_partial = dot(activations, basis_a).astype(bf16)
    act_blocks = act_partial.reshape(tok, 8, feats).transpose(1, 0, 2).reshape(8, tok * feats // units, units)
    packed = jnp.concatenate([jnp.broadcast_to(out_grads, (8, rows, units)), act_blocks], axis=1)
    packed = exchange(packed, ("x", "zl"))
    grad_rows = packed[:, :rows].reshape(tokens, units)
    act_own = jnp.sum(packed[:, rows:].astype(f32), axis=0).astype(bf16).reshape(tok, feats)

    g_mine = jnp.stack([g_own, g_far])
    g_zl = flip(g_mine, "zl")
    g_zz = lax.ppermute(g_mine, ("zl", "zh"), [(i, 3 - i) for i in range(4)])

    far = flip(dot(grad_rows, g_far).astype(bf16), "c")
    near = dot(grad_rows, g_own) + far.astype(f32)
    parts = exchange(near.astype(bf16).reshape(4, tokens // 4, half), "y")
    part = jnp.sum(parts.astype(f32), axis=0)
    part = part + flip(part.astype(bf16), "zh").astype(f32)
    grad_projected = spread(part.astype(bf16), "y", 4).reshape(tokens, half)

    act_zh = order(zh, act_own[None], flip(act_own, "zh")[None], 0)
    act_y = [act_zh] + [shift(act_zh, "y", k) for k in (1, 3, 2)]
    act_y = jnp.stack(act_y)
    y = lax.axis_index("y")
    x = lax.axis_index("x")
    order_of = jnp.array([0, 1, 3, 2])
    act_y = jnp.take(act_y, order_of[(jnp.arange(4) - y) % 4], axis=0)
    act_cols = act_y.reshape(8 * tok, feats)
    act_zl = order(zl, act_cols, flip(act_cols, "zl"), 1)
    act_x = jnp.stack([act_zl] + [shift(act_zl, "x", k) for k in (1, 3, 2)])
    act_x = jnp.take(act_x, order_of[(jnp.arange(4) - x) % 4], axis=0)
    act_far = flip(act_x, "c")
    act_all = order(c, act_x.reshape(4, 8, 1, tok, 2 * feats), act_far.reshape(4, 8, 1, tok, 2 * feats), 2)
    act_all = act_all.transpose(1, 2, 3, 0, 4).reshape(tokens, di)

    quarter = feats // 4
    a_part = lax.dynamic_slice_in_dim(basis_a.reshape(2, 2, quarter, di), zh, 1, 0)[0]
    a_part = lax.dynamic_slice_in_dim(a_part, c, 1, 0)[0]
    a_part = permute_all(a_part, lambda x, zl, y, zh, c: (y, zl, x, zh, c))
    a_pair = jnp.stack([a_part, flip(a_part, "zl")])
    a_far = flip(a_pair, "c")
    a_rows = order(c, a_pair, a_far, 1).reshape(4 * quarter, di)

    spectrum_all = lax.all_gather(spectrum_a, ("y", "zh", "c"), axis=0, tiled=True)
    spectrum_own = lax.dynamic_slice_in_dim(spectrum_g, c * half, half, 0)
    rotated = contract_rows(grad_projected, act_all) / tokens
    scaled = (rotated / (spectrum_own[:, None] * spectrum_all[None, :] + damping)).astype(bf16)
    turned = lax.dot_general(
        scaled, a_rows, (((1,), (1,)), ((), ())), preferred_element_type=f32
    ).astype(bf16)
    wide = turned.shape[1] // 2
    w = jnp.stack([turned[:, :wide], flip(turned[:, wide:], "zl")])
    w = spread(w, "y", 4)
    w_far = flip(w, "c")

    near_zl = flip(g_zz[0], "zl")
    near_zz = lax.ppermute(g_zl[1], ("zl", "zh"), [(i, 3 - i) for i in range(4)])
    g_zh = jnp.stack([near_zl, near_zz])
    table = [[g_mine, g_zl], [g_zh, g_zz]]

    shares = []
    for dzh in range(2):
        total = None
        for dzl in range(2):
            for core, held in enumerate((w, w_far)):
                term = jnp.einsum("un,ynj->yuj", table[dzh][dzl][core], held[:, dzl], preferred_element_type=f32)
                total = term if total is None else total + term
        shares.append(total.astype(bf16))
    shares = exchange(jnp.concatenate(shares, axis=1), "x")
    share = jnp.sum(shares.astype(f32), axis=0).astype(bf16)
    update = order(zh, share[:units], flip(share[units:], "zh"), 1)

    turn = lambda x, zl, y, zh, c: (y, zh, x, zl, c)
    grad_turned = permute_all(out_grads, turn)
    grad_cols = lax.all_gather(grad_turned, ("y", "zh"), axis=0, tiled=True)
    grad_cols = lax.all_gather(grad_cols, "c", axis=1, tiled=True)
    factor_g_new = decay_rate * factor_g + rate * contract_rows(grad_rows, grad_cols)
    act_rows = lax.all_gather(activations, ("y", "zh", "c"), axis=0, tiled=True)
    act_turned = permute_all(activations, turn)
    act_part = lax.all_gather(act_turned, ("x", "zl", "c"), axis=0, tiled=True)
    narrow = factor_a.shape[1]
    act_part = lax.dynamic_slice_in_dim(act_part, c * narrow, narrow, 1)
    factor_a_new = decay_rate * factor_a + rate * contract_rows(act_rows, act_part)
    return update, factor_a_new, factor_g_new


def solution(mesh):
    fine = Mesh(mesh.devices.reshape(SIZES), NAMES)
    dp = ("x", "zl")
    mp = ("y", "zh", "c")
    placed = (
        P(dp, mp),
        P(mp, dp),
        P(dp, mp),
        P(mp, dp),
        P(dp, None),
        P(mp, dp),
        P(mp),
        P(dp),
    )
    return jax.shard_map(
        shards,
        mesh=fine,
        in_specs=placed,
        out_specs=(P(mp, dp), P(dp, mp), P(mp, dp)),
        check_vma=False,
    )
```

```python
import jax
import jax.numpy as jnp
from jax import lax
from jax.sharding import Mesh, PartitionSpec as P

decay_rate = 0.95
damping = 0.25
NAMES = ("x", "zl", "y", "zh", "c")
SIZES = (4, 2, 4, 2, 2)
f32 = jnp.float32
bf16 = jnp.bfloat16


def permute_all(value, target):
    pairs = []
    source = 0
    for x in range(4):
        for zl in range(2):
            for y in range(4):
                for zh in range(2):
                    for c in range(2):
                        tx, tzl, ty, tzh, tc = target(x, zl, y, zh, c)
                        dest = (((tx % 4 * 2 + tzl) * 4 + ty % 4) * 2 + tzh) * 2 + tc
                        pairs.append((source, dest))
                        source += 1
    return lax.ppermute(value, NAMES, pairs)


def flip(value, axis):
    return lax.ppermute(value, axis, [(0, 1), (1, 0)])


def flip_z(value):
    return lax.ppermute(value, ("zl", "zh"), [(i, 3 - i) for i in range(4)])


def exchange(blocks, axis):
    return lax.all_to_all(blocks, axis, split_axis=0, concat_axis=0, tiled=True)


def spread(block, axis, n):
    return exchange(jnp.broadcast_to(block, (n,) + block.shape), axis)


def after(value, *deps):
    return lax.optimization_barrier((value,) + deps)[0]


def shift(value, axis, by):
    return lax.ppermute(value, axis, [((i + by) % 4, i) for i in range(4)])


def around(block, axis):
    return [block] + [shift(block, axis, by) for by in STEPS[1:]]


STEPS = (0, 1, 3, 2)


def by_place(blocks, place):
    out = jnp.zeros((4,) + blocks[0].shape, blocks[0].dtype)
    for step, block in zip(STEPS, blocks):
        out = lax.dynamic_update_index_in_dim(out, block, (place + step) % 4, 0)
    return out


def by_distance(rows, place):
    wide = rows.shape[1] // 4
    out = jnp.zeros_like(rows)
    for slot, step in enumerate(STEPS):
        block = lax.dynamic_slice_in_dim(rows, (place + step) % 4 * wide, wide, 1)
        out = lax.dynamic_update_slice(out, block, (0, slot * wide))
    return out


def dot(a, b):
    return jnp.dot(a, b, preferred_element_type=f32)


def dot_rows(left, right):
    return lax.dot_general(left, right, (((0,), (0,)), ((), ())), preferred_element_type=f32)


def dot_cols(left, right):
    return lax.dot_general(left, right, (((1,), (1,)), ((), ())), preferred_element_type=f32)


def order(index, own, other, axis):
    return jnp.where(
        index == 0,
        jnp.concatenate([own, other], axis=axis),
        jnp.concatenate([other, own], axis=axis),
    )


def shards(out_grads, activations, factor_a, factor_g, basis_a, basis_g, spectrum_a, spectrum_g):
    zl = lax.axis_index("zl")
    zh = lax.axis_index("zh")
    c = lax.axis_index("c")
    x = lax.axis_index("x")
    y = lax.axis_index("y")
    tokens = out_grads.shape[0] * 8
    rows, units = out_grads.shape
    tok, feats = activations.shape
    di = basis_a.shape[1]
    half = basis_g.shape[1] // 2
    quarter = feats // 4
    rate = (1.0 - decay_rate) / tokens
    turn = lambda x, zl, y, zh, c: (y, zh, x, zl, c)

    act_partial = dot(activations, basis_a).astype(bf16)
    act_parts = exchange(act_partial.reshape(tok, 8, feats).transpose(1, 0, 2), ("x", "zl"))
    grad_pair = order(zl, out_grads, flip(out_grads, "zl"), 0)
    grad_pair = after(grad_pair, act_parts)
    grad_x = around(grad_pair, "x")

    act_own = jnp.sum(after(act_parts, grad_pair).astype(f32), axis=0).astype(bf16)
    act_zl = order(zl, act_own, flip(act_own, "zl"), 1)
    act_zl = jnp.concatenate([act_zl, activations.reshape(tok // 2, 2 * feats)])
    act_zh = order(zh, act_zl[None], flip(act_zl, "zh")[None], 0)
    act_y = [act_zh] + [shift(act_zh, "y", k) for k in STEPS[1:]]

    g_own = lax.dynamic_slice_in_dim(basis_g, c * half, half, 1)
    g_far = lax.dynamic_slice_in_dim(basis_g, (1 - c) * half, half, 1)
    own_sent = after(g_own, act_zh)
    own_zl = flip(own_sent, "zl")
    own_zz = flip_z(own_sent)

    ready = after(tuple(grad_x), act_zh)
    grad_rows = by_place(ready, x).reshape(tokens, units)
    far = flip(dot(grad_rows, g_far).astype(bf16), "c")
    near = (dot(grad_rows, g_own) + far.astype(f32)).astype(bf16).reshape(4, tokens // 4, half)

    a_part = lax.dynamic_slice_in_dim(basis_a.reshape(2, 2, quarter, di), zh, 1, 0)[0]
    a_part = lax.dynamic_slice_in_dim(a_part, c, 1, 0)[0]
    a_part = permute_all(after(a_part, *grad_x), lambda x, zl, y, zh, c: (x - y, zl, y, zh, c))

    near = after(near, *act_y)
    parts = exchange(near, "y")
    act_y = by_place(act_y, y)
    act_cols = act_y[:, :, :tok].reshape(8 * tok, 2 * feats)
    a_zl = flip(after(a_part, own_zl, near), "zl")
    part = jnp.sum(parts.astype(f32), axis=0)
    act_x = around(act_cols, "x")
    part_sent = after(part.astype(bf16), own_zl, own_zz, a_zl, act_x[1], act_x[2])
    a_pair = jnp.stack([a_part, a_zl])
    a_rows = order(c, a_pair, flip(after(a_pair, part_sent), "c"), 1).reshape(4 * quarter, di)
    a_rows = by_distance(a_rows, x)
    grad_turned = permute_all(after(out_grads, part_sent), turn)
    act_turned = permute_all(after(activations, part_sent), turn)
    spectrum_all = spread(after(spectrum_a, part_sent), ("y", "zh", "c"), 16).reshape(1, di)
    part = (part + flip(part_sent, "zh").astype(f32)).astype(bf16)
    part = after(part, spectrum_all)
    part = part.reshape(2, 2, tok, half).transpose(1, 0, 2, 3)
    part = jnp.where(c == 0, part, part[::-1])
    part = jnp.broadcast_to(part.reshape(2, 2 * tok, half), (4, 2, 2 * tok, half))
    grads = exchange(part, "y").reshape(tokens, half)

    far_sent = after(g_far, part)
    far_zl = flip(far_sent, "zl")
    far_zz = flip_z(far_sent)
    act_all = jnp.zeros((4, 2, 2 * tok, di), bf16)
    for slot, block in enumerate(act_x):
        act_all = lax.dynamic_update_slice(
            act_all, block.reshape(4, 1, 2 * tok, 2 * feats), (0, 0, 0, slot * 2 * feats)
        )
    act_all = lax.dynamic_update_slice(act_all, flip(act_all[:, :1], "c"), (0, 1, 0, 0)).reshape(tokens, di)
    grads = after(grads, far_zl, far_zz, a_rows)
    far_zh = flip_z(far_zl)
    turned_zh = flip(after(grad_turned, far_zl), "zh")
    own_zh = flip(after(own_zz, far_zl), "zl")

    spectrum_own = lax.dynamic_slice_in_dim(spectrum_g, c * half, half, 0)[:, None]
    spectrum_all = by_distance(spectrum_all, x)
    rotated = dot_rows(grads, act_all) / tokens
    scaled = (rotated / (spectrum_own * spectrum_all + damping)).astype(bf16)
    turned = dot_cols(a_rows, scaled).astype(bf16)
    grad_turned = order(zh, grad_turned, turned_zh, 0)
    cols = spread(after(grad_turned, grads), "y", 4).reshape(tokens, units)
    wide = 2 * quarter
    w = jnp.concatenate([turned[:wide], flip(turned[wide:], "zl")], axis=1)
    w = after(w, far_zh, own_zh, cols)

    g_near = jnp.concatenate([jnp.concatenate([g_own, own_zl], axis=1), jnp.concatenate([own_zh, own_zz], axis=1)])
    g_away = jnp.concatenate([jnp.concatenate([g_far, far_zl], axis=1), jnp.concatenate([far_zh, far_zz], axis=1)])
    first, last = shift(w, "y", 1), shift(w, "y", 3)
    opposite = shift(first[:quarter], "y", 1), shift(last[quarter:], "y", 3)

    def rotate(unit):
        return (dot_cols(unit, g_near) + dot_cols(flip(unit, "c"), g_away)).astype(bf16)

    def send(made, k):
        return permute_all(made, lambda x, zl, y, zh, c: (x + y + k, zl, y, zh, c))

    made = rotate(w)
    shares = [send(made, 0)]
    first, last = after((first, last), made)
    made_first, made_last = rotate(first), rotate(last)
    shares += [send(made_first, 1), send(made_last, 3)]
    opposite = jnp.concatenate(after(opposite, made_first, made_last, shares[0]))
    made = rotate(opposite)
    shares.append(send(made, 2))
    share = sum(s.astype(f32) for s in shares).astype(bf16)
    cols = order(c, cols, flip(after(cols, first, last), "c"), 1)
    factor_g_new = decay_rate * factor_g + rate * dot_rows(grad_rows, cols)
    share = after(share, factor_g_new)
    update = order(zh, share[:, :units], flip(share[:, units:], "zh"), 0).T
    act_rows = act_y[:, :, tok:].reshape(8, 1, tok, feats)
    act_rows = order(c, act_rows, flip(after(act_rows, grads), "c"), 1).reshape(tokens, feats)
    act_part = spread(after(act_turned, made), ("x", "zl", "c"), 16).reshape(tokens, feats)
    narrow = factor_a.shape[1]
    act_part = lax.dynamic_slice_in_dim(act_part, c * narrow, narrow, 1)
    factor_a_new = decay_rate * factor_a + rate * dot_rows(act_rows, act_part)
    return update, factor_a_new, factor_g_new


def solution(mesh):
    fine = Mesh(mesh.devices.reshape(SIZES), NAMES)
    dp = ("x", "zl")
    mp = ("y", "zh", "c")
    placed = (
        P(dp, mp),
        P(mp, dp),
        P(dp, mp),
        P(mp, dp),
        P(dp, None),
        P(mp, dp),
        P(mp),
        P(dp),
    )
    return jax.shard_map(
        shards,
        mesh=fine,
        in_specs=placed,
        out_specs=(P(mp, dp), P(dp, mp), P(mp, dp)),
        check_vma=False,
    )
```

```python
import jax
import jax.numpy as jnp
from jax import lax
from jax.sharding import Mesh, PartitionSpec as P

decay_rate = 0.95
damping = 0.25
NAMES = ("x", "zl", "y", "zh", "c")
SIZES = (4, 2, 4, 2, 2)
f32 = jnp.float32
bf16 = jnp.bfloat16


def permute_all(value, target):
    pairs = []
    source = 0
    for x in range(4):
        for zl in range(2):
            for y in range(4):
                for zh in range(2):
                    for c in range(2):
                        tx, tzl, ty, tzh, tc = target(x, zl, y, zh, c)
                        dest = (((tx % 4 * 2 + tzl) * 4 + ty % 4) * 2 + tzh) * 2 + tc
                        pairs.append((source, dest))
                        source += 1
    return lax.ppermute(value, NAMES, pairs)


def flip(value, axis):
    return lax.ppermute(value, axis, [(0, 1), (1, 0)])


def flip_z(value):
    return lax.ppermute(value, ("zl", "zh"), [(i, 3 - i) for i in range(4)])


def exchange(blocks, axis):
    return lax.all_to_all(blocks, axis, split_axis=0, concat_axis=0, tiled=True)


def spread(block, axis, n):
    return exchange(jnp.broadcast_to(block, (n,) + block.shape), axis)


def after(value, *deps):
    return lax.optimization_barrier((value,) + deps)[0]


def shift(value, axis, by):
    return lax.ppermute(value, axis, [((i + by) % 4, i) for i in range(4)])


def around(block, axis):
    return [block] + [shift(block, axis, by) for by in STEPS[1:]]


STEPS = (0, 1, 3, 2)


def by_place(blocks, place):
    out = jnp.zeros((4,) + blocks[0].shape, blocks[0].dtype)
    for step, block in zip(STEPS, blocks):
        out = lax.dynamic_update_index_in_dim(out, block, (place + step) % 4, 0)
    return out


def by_distance(rows, place):
    wide = rows.shape[1] // 4
    out = jnp.zeros_like(rows)
    for slot, step in enumerate(STEPS):
        block = lax.dynamic_slice_in_dim(rows, (place + step) % 4 * wide, wide, 1)
        out = lax.dynamic_update_slice(out, block, (0, slot * wide))
    return out


def dot(a, b):
    return jnp.dot(a, b, preferred_element_type=f32)


def dot_rows(left, right):
    return lax.dot_general(left, right, (((0,), (0,)), ((), ())), preferred_element_type=f32)


def dot_cols(left, right):
    return lax.dot_general(left, right, (((1,), (1,)), ((), ())), preferred_element_type=f32)


def order(index, own, other, axis):
    return jnp.where(
        index == 0,
        jnp.concatenate([own, other], axis=axis),
        jnp.concatenate([other, own], axis=axis),
    )


def shards(out_grads, activations, factor_a, factor_g, basis_a, basis_g, spectrum_a, spectrum_g):
    zl = lax.axis_index("zl")
    zh = lax.axis_index("zh")
    c = lax.axis_index("c")
    x = lax.axis_index("x")
    y = lax.axis_index("y")
    tokens = out_grads.shape[0] * 8
    rows, units = out_grads.shape
    tok, feats = activations.shape
    di = basis_a.shape[1]
    half = basis_g.shape[1] // 2
    quarter = feats // 4
    rate = (1.0 - decay_rate) / tokens
    turn = lambda x, zl, y, zh, c: (y, zh, x, zl, c)

    act_partial = dot(activations, basis_a).astype(bf16)
    act_parts = exchange(act_partial.reshape(tok, 8, feats).transpose(1, 0, 2), ("x", "zl"))
    grad_pair = order(zl, out_grads, flip(out_grads, "zl"), 0)
    grad_pair = after(grad_pair, act_parts)
    grad_x = around(grad_pair, "x")

    act_own = jnp.sum(after(act_parts, grad_pair).astype(f32), axis=0).astype(bf16)
    act_zl = order(zl, act_own, flip(act_own, "zl"), 1)
    act_zl = jnp.concatenate([act_zl, activations.reshape(tok // 2, 2 * feats)])
    act_zh = order(zh, act_zl[None], flip(act_zl, "zh")[None], 0)
    act_y = [act_zh] + [shift(act_zh, "y", k) for k in STEPS[1:]]

    g_own = lax.dynamic_slice_in_dim(basis_g, c * half, half, 1)
    g_far = lax.dynamic_slice_in_dim(basis_g, (1 - c) * half, half, 1)
    own_sent = after(g_own, act_zh)
    own_zl = flip(own_sent, "zl")
    own_zz = flip_z(own_sent)

    ready = after(tuple(grad_x), act_zh)
    grad_rows = by_place(ready, x).reshape(tokens, units)
    far = flip(dot(grad_rows, g_far).astype(bf16), "c")
    near = (dot(grad_rows, g_own) + far.astype(f32)).astype(bf16).reshape(4, tokens // 4, half)

    a_part = lax.dynamic_slice_in_dim(basis_a.reshape(2, 2, quarter, di), zh, 1, 0)[0]
    a_part = lax.dynamic_slice_in_dim(a_part, c, 1, 0)[0]
    a_part = permute_all(after(a_part, *grad_x), lambda x, zl, y, zh, c: (x - y, zl, y, zh, c))

    near = after(near, *act_y)
    parts = exchange(near, "y")
    act_y = by_place(act_y, y)
    act_cols = act_y[:, :, :tok].reshape(8 * tok, 2 * feats)
    a_zl = flip(after(a_part, own_zl, near), "zl")
    part = jnp.sum(parts.astype(f32), axis=0)
    act_x = around(act_cols, "x")
    part_sent = after(part.astype(bf16), own_zl, own_zz, a_zl, act_x[1], act_x[2])
    a_pair = jnp.stack([a_part, a_zl])
    a_rows = order(c, a_pair, flip(after(a_pair, part_sent), "c"), 1).reshape(4 * quarter, di)
    a_rows = by_distance(a_rows, x)
    spectrum_all = spread(after(spectrum_a, part_sent), ("y", "zh", "c"), 16).reshape(1, di)
    part = (part + flip(part_sent, "zh").astype(f32)).astype(bf16)
    part = after(part, spectrum_all)
    part = part.reshape(2, 2, tok, half).transpose(1, 0, 2, 3)
    part = jnp.where(c == 0, part, part[::-1])
    part = jnp.broadcast_to(part.reshape(2, 2 * tok, half), (4, 2, 2 * tok, half))
    grads = exchange(part, "y").reshape(tokens, half)

    far_sent = after(g_far, part)
    far_zl = flip(far_sent, "zl")
    far_zz = flip_z(far_sent)
    act_turned = permute_all(after(activations, part), turn)
    act_x = after(tuple(act_x), act_turned)
    act_all = jnp.zeros((4, 2, 2 * tok, di), bf16)
    for slot, block in enumerate(act_x):
        act_all = lax.dynamic_update_slice(
            act_all, block.reshape(4, 1, 2 * tok, 2 * feats), (0, 0, 0, slot * 2 * feats)
        )
    act_all = lax.dynamic_update_slice(act_all, flip(act_all[:, :1], "c"), (0, 1, 0, 0)).reshape(tokens, di)
    grads = after(grads, far_zl, far_zz, a_rows)
    far_zh = flip_z(far_zl)
    own_zh = flip(after(own_zz, far_zl), "zl")

    spectrum_own = lax.dynamic_slice_in_dim(spectrum_g, c * half, half, 0)[:, None]
    spectrum_all = by_distance(spectrum_all, x)
    rotated = dot_rows(grads, act_all) / tokens
    scaled = (rotated / (spectrum_own * spectrum_all + damping)).astype(bf16)
    turned = dot_cols(a_rows, scaled).astype(bf16)
    wide = 2 * quarter
    w = jnp.concatenate([turned[:wide], flip(turned[wide:], "zl")], axis=1)
    w = after(w, far_zh, own_zh)
    grad_turned = permute_all(after(out_grads, w), turn)

    g_near = jnp.concatenate([jnp.concatenate([g_own, own_zl], axis=1), jnp.concatenate([own_zh, own_zz], axis=1)])
    g_away = jnp.concatenate([jnp.concatenate([g_far, far_zl], axis=1), jnp.concatenate([far_zh, far_zz], axis=1)])
    first, last = shift(w, "y", 1), shift(w, "y", 3)
    opposite = shift(first[:quarter], "y", 1), shift(last[quarter:], "y", 3)

    def rotate(unit):
        return (dot_cols(unit, g_near) + dot_cols(flip(unit, "c"), g_away)).astype(bf16)

    def send(made, k):
        return permute_all(made, lambda x, zl, y, zh, c: (x + y + k, zl, y, zh, c))

    made = rotate(w)
    shares = [send(made, 0)]
    first, last = after((first, last), made)
    made_first, made_last = rotate(first), rotate(last)
    shares += [send(made_first, 1), send(made_last, 3)]
    opposite = jnp.concatenate(after(opposite, made_first, made_last, shares[0]))
    made = rotate(opposite)
    shares.append(send(made, 2))
    share = sum(s.astype(f32) for s in shares).astype(bf16)
    cols = spread(after(grad_turned, made_last), ("y", "zh"), 8).reshape(tokens, units)
    cols = after(cols, shares[1], shares[2])
    cols = order(c, cols, flip(cols, "c"), 1)
    factor_g_new = decay_rate * factor_g + rate * dot_rows(grad_rows, cols)
    share = after(share, factor_g_new)
    update = order(zh, share[:, :units], flip(share[:, units:], "zh"), 0).T
    act_rows = act_y[:, :, tok:].reshape(8, 1, tok, feats)
    act_rows = order(c, act_rows, flip(after(act_rows, grads), "c"), 1).reshape(tokens, feats)
    act_part = spread(after(act_turned, made), ("x", "zl", "c"), 16).reshape(tokens, feats)
    narrow = factor_a.shape[1]
    act_part = lax.dynamic_slice_in_dim(act_part, c * narrow, narrow, 1)
    factor_a_new = decay_rate * factor_a + rate * dot_rows(act_rows, act_part)
    return update, factor_a_new, factor_g_new


def solution(mesh):
    fine = Mesh(mesh.devices.reshape(SIZES), NAMES)
    dp = ("x", "zl")
    mp = ("y", "zh", "c")
    placed = (
        P(dp, mp),
        P(mp, dp),
        P(dp, mp),
        P(mp, dp),
        P(dp, None),
        P(mp, dp),
        P(mp),
        P(dp),
    )
    return jax.shard_map(
        shards,
        mesh=fine,
        in_specs=placed,
        out_specs=(P(mp, dp), P(dp, mp), P(mp, dp)),
        check_vma=False,
    )
```

```python
import jax
import jax.numpy as jnp
from jax import lax
from jax.sharding import Mesh, PartitionSpec as P

decay_rate = 0.95
damping = 0.25
NAMES = ("x", "zl", "y", "zh", "c")
SIZES = (4, 2, 4, 2, 2)
f32 = jnp.float32
bf16 = jnp.bfloat16


def permute_all(value, target):
    pairs = []
    source = 0
    for x in range(4):
        for zl in range(2):
            for y in range(4):
                for zh in range(2):
                    for c in range(2):
                        tx, tzl, ty, tzh, tc = target(x, zl, y, zh, c)
                        dest = (((tx % 4 * 2 + tzl) * 4 + ty % 4) * 2 + tzh) * 2 + tc
                        pairs.append((source, dest))
                        source += 1
    return lax.ppermute(value, NAMES, pairs)


def flip(value, axis):
    return lax.ppermute(value, axis, [(0, 1), (1, 0)])


def flip_z(value):
    return lax.ppermute(value, ("zl", "zh"), [(i, 3 - i) for i in range(4)])


def exchange(blocks, axis):
    return lax.all_to_all(blocks, axis, split_axis=0, concat_axis=0, tiled=True)


def spread(block, axis, n):
    return exchange(jnp.broadcast_to(block, (n,) + block.shape), axis)


def after(value, *deps):
    return lax.optimization_barrier((value,) + deps)[0]


def shift(value, axis, by):
    return lax.ppermute(value, axis, [((i + by) % 4, i) for i in range(4)])


def around(block, axis):
    return [block] + [shift(block, axis, by) for by in STEPS[1:]]


STEPS = (0, 1, 3, 2)


def by_place(blocks, place):
    out = jnp.zeros((4,) + blocks[0].shape, blocks[0].dtype)
    for step, block in zip(STEPS, blocks):
        out = lax.dynamic_update_index_in_dim(out, block, (place + step) % 4, 0)
    return out


def by_distance(rows, place):
    wide = rows.shape[1] // 4
    out = jnp.zeros_like(rows)
    for slot, step in enumerate(STEPS):
        block = lax.dynamic_slice_in_dim(rows, (place + step) % 4 * wide, wide, 1)
        out = lax.dynamic_update_slice(out, block, (0, slot * wide))
    return out


def dot(a, b):
    return jnp.dot(a, b, preferred_element_type=f32)


def dot_rows(left, right):
    return lax.dot_general(left, right, (((0,), (0,)), ((), ())), preferred_element_type=f32)


def dot_cols(left, right):
    return lax.dot_general(left, right, (((1,), (1,)), ((), ())), preferred_element_type=f32)


def order(index, own, other, axis):
    return jnp.where(
        index == 0,
        jnp.concatenate([own, other], axis=axis),
        jnp.concatenate([other, own], axis=axis),
    )


def shards(out_grads, activations, factor_a, factor_g, basis_a, basis_g, spectrum_a, spectrum_g):
    zl = lax.axis_index("zl")
    zh = lax.axis_index("zh")
    c = lax.axis_index("c")
    x = lax.axis_index("x")
    y = lax.axis_index("y")
    tokens = out_grads.shape[0] * 8
    rows, units = out_grads.shape
    tok, feats = activations.shape
    di = basis_a.shape[1]
    half = basis_g.shape[1] // 2
    quarter = feats // 4
    rate = (1.0 - decay_rate) / tokens
    turn = lambda x, zl, y, zh, c: (y, zh, x, zl, c)

    act_partial = dot(activations, basis_a).astype(bf16)
    act_parts = exchange(act_partial.reshape(tok, 8, feats).transpose(1, 0, 2), ("x", "zl"))
    grad_pair = order(zl, out_grads, flip(out_grads, "zl"), 0)
    grad_pair = after(grad_pair, act_parts)
    grad_x = around(grad_pair, "x")

    act_own = jnp.sum(after(act_parts, grad_pair).astype(f32), axis=0).astype(bf16)
    act_zl = order(zl, act_own, flip(act_own, "zl"), 1)
    act_zl = jnp.concatenate([act_zl, activations.reshape(tok // 2, 2 * feats)])
    act_zh = order(zh, act_zl[None], flip(act_zl, "zh")[None], 0)
    act_y = [act_zh] + [shift(act_zh, "y", k) for k in STEPS[1:]]

    g_own = lax.dynamic_slice_in_dim(basis_g, c * half, half, 1)
    g_far = lax.dynamic_slice_in_dim(basis_g, (1 - c) * half, half, 1)
    own_sent = after(g_own, act_zh)
    own_zl = flip(own_sent, "zl")
    own_zz = flip_z(own_sent)

    ready = after(tuple(grad_x), act_zh)
    grad_rows = by_place(ready, x).reshape(tokens, units)
    far = flip(dot(grad_rows, g_far).astype(bf16), "c")
    near = (dot(grad_rows, g_own) + far.astype(f32)).astype(bf16).reshape(4, tokens // 4, half)

    a_part = lax.dynamic_slice_in_dim(basis_a.reshape(2, 2, quarter, di), zh, 1, 0)[0]
    a_part = lax.dynamic_slice_in_dim(a_part, c, 1, 0)[0]
    a_part = permute_all(after(a_part, *grad_x), lambda x, zl, y, zh, c: (x - y, zl, y, zh, c))

    near = after(near, *act_y)
    parts = exchange(near, "y")
    act_y = by_place(act_y, y)
    act_cols = act_y[:, :, :tok].reshape(8 * tok, 2 * feats)
    a_zl = flip(after(a_part, own_zl, near), "zl")
    part = jnp.sum(parts.astype(f32), axis=0)
    act_x = around(act_cols, "x")
    part_sent = after(part.astype(bf16), own_zl, own_zz, a_zl, act_x[1], act_x[2])
    a_pair = jnp.stack([a_part, a_zl])
    a_rows = order(c, a_pair, flip(after(a_pair, part_sent), "c"), 1).reshape(4 * quarter, di)
    a_rows = by_distance(a_rows, x)
    spectrum_all = spread(after(spectrum_a, part_sent), ("y", "zh", "c"), 16).reshape(1, di)
    part = (part + flip(part_sent, "zh").astype(f32)).astype(bf16)
    part = after(part, spectrum_all)
    part = part.reshape(2, 2, tok, half).transpose(1, 0, 2, 3)
    part = jnp.where(c == 0, part, part[::-1])
    part = jnp.broadcast_to(part.reshape(2, 2 * tok, half), (4, 2, 2 * tok, half))
    grads = exchange(part, "y").reshape(tokens, half)

    far_sent = after(g_far, part)
    far_zl = flip(far_sent, "zl")
    far_zz = flip_z(far_sent)
    act_turned = permute_all(after(activations, part), turn)
    act_x = after(tuple(act_x), act_turned)
    act_all = jnp.zeros((4, 2, 2 * tok, di), bf16)
    for slot, block in enumerate(act_x):
        act_all = lax.dynamic_update_slice(
            act_all, block.reshape(4, 1, 2 * tok, 2 * feats), (0, 0, 0, slot * 2 * feats)
        )
    act_all = lax.dynamic_update_slice(act_all, flip(act_all[:, :1], "c"), (0, 1, 0, 0)).reshape(tokens, di)
    grads = after(grads, far_zl, far_zz, a_rows)
    far_zh = flip_z(far_zl)
    grad_turned = permute_all(after(out_grads, act_turned), turn)
    turned_zh = flip(after(grad_turned, far_zl), "zh")
    own_zh = flip(after(own_zz, far_zl), "zl")

    spectrum_own = lax.dynamic_slice_in_dim(spectrum_g, c * half, half, 0)[:, None]
    spectrum_all = by_distance(spectrum_all, x)
    rotated = dot_rows(grads, act_all) / tokens
    scaled = (rotated / (spectrum_own * spectrum_all + damping)).astype(bf16)
    turned = dot_cols(a_rows, scaled).astype(bf16)
    grad_turned = order(zh, grad_turned, turned_zh, 0)
    cols = spread(after(grad_turned, grads), "y", 4).reshape(tokens, units)
    wide = 2 * quarter
    w = jnp.concatenate([turned[:wide], flip(turned[wide:], "zl")], axis=1)
    w = after(w, far_zh, own_zh, cols)

    g_near = jnp.concatenate([jnp.concatenate([g_own, own_zl], axis=1), jnp.concatenate([own_zh, own_zz], axis=1)])
    g_away = jnp.concatenate([jnp.concatenate([g_far, far_zl], axis=1), jnp.concatenate([far_zh, far_zz], axis=1)])
    first, last = shift(w, "y", 1), shift(w, "y", 3)
    opposite = shift(first[:quarter], "y", 1), shift(last[quarter:], "y", 3)

    def rotate(unit):
        return (dot_cols(unit, g_near) + dot_cols(flip(unit, "c"), g_away)).astype(bf16)

    def send(made, k):
        return permute_all(made, lambda x, zl, y, zh, c: (x + y + k, zl, y, zh, c))

    made = rotate(w)
    shares = [send(made, 0)]
    first, last = after((first, last), made)
    made_first, made_last = rotate(first), rotate(last)
    shares += [send(made_first, 1), send(made_last, 3)]
    opposite = jnp.concatenate(after(opposite, made_first, made_last, shares[0]))
    made = rotate(opposite)
    shares.append(send(made, 2))
    share = sum(s.astype(f32) for s in shares).astype(bf16)
    cols = order(c, cols, flip(after(cols, first, last), "c"), 1)
    factor_g_new = decay_rate * factor_g + rate * dot_rows(grad_rows, cols)
    share = after(share, factor_g_new)
    update = order(zh, share[:, :units], flip(share[:, units:], "zh"), 0).T
    act_rows = act_y[:, :, tok:].reshape(8, 1, tok, feats)
    act_rows = order(c, act_rows, flip(after(act_rows, grads), "c"), 1).reshape(tokens, feats)
    act_part = spread(after(act_turned, made), ("x", "zl", "c"), 16).reshape(tokens, feats)
    narrow = factor_a.shape[1]
    act_part = lax.dynamic_slice_in_dim(act_part, c * narrow, narrow, 1)
    factor_a_new = decay_rate * factor_a + rate * dot_rows(act_rows, act_part)
    return update, factor_a_new, factor_g_new


def solution(mesh):
    fine = Mesh(mesh.devices.reshape(SIZES), NAMES)
    dp = ("x", "zl")
    mp = ("y", "zh", "c")
    placed = (
        P(dp, mp),
        P(mp, dp),
        P(dp, mp),
        P(mp, dp),
        P(dp, None),
        P(mp, dp),
        P(mp),
        P(dp),
    )
    return jax.shard_map(
        shards,
        mesh=fine,
        in_specs=placed,
        out_specs=(P(mp, dp), P(dp, mp), P(mp, dp)),
        check_vma=False,
    )
```
